32 devices in a mesh: wide: 8 (over y, x, core), narrow: 4 (over z).
Axes of the slice: x: 2, y: 2, z: 4, core: 2. Of those that a mesh axis runs over, the one named last changes fastest.
Arguments:
- pair_tokens: bfloat16 [32, 2, 128, 768], P(('wide', 'narrow')), may hold values from -6 to 6
- expert_ids: int32 [32, 256, 2], P(('wide', 'narrow')), may hold values from 0 to 7, all different within a row; in each aligned block of 256 rows (0 to 255, 256 to 511, ..., all dimensions but the last counted through in order) at most 68 rows name the same one
- positive: int32 [32], replicated, may hold values from 0 to 31, each once
- w_qkv: bfloat16 [768, 2304], replicated, may hold values from -0.21875 to 0.21875
- w_out: bfloat16 [768, 768], replicated, may hold values from -0.21875 to 0.21875
- w_router: bfloat16 [768, 8], replicated, may hold values from -0.21875 to 0.21875
- w_up: bfloat16 [8, 768, 3072], P('wide', None, 'narrow'), may hold values from -0.21875 to 0.21875
- w_down: bfloat16 [8, 3072, 768], P('wide', 'narrow'), may hold values from -0.109375 to 0.109375
Outputs:
- grad_up: float32 [8, 768, 3072], P('wide', None, 'narrow')
- grad_down: float32 [8, 3072, 768], P('wide', 'narrow')
The draws below stay inside these ranges and needn't reach their ends.
Inputs may be any that keep to these rules, and one draw needn't show every extreme that they name: `expert_ids`: the two experts of a token differ. Among the 256 tokens of one device no expert is named more than 68 times, and in every draw some device names some expert exactly 68 times. Each document is the positive of exactly one query.
All inputs are finite; a program needn't handle non-finite values.
Results may differ from the reference program's by a relative error of at most 0.023.
Values may be sent and summed in bfloat16 or wider, within the bound.
No kernel may reach another device: no remote copies, remote signals or barrier semaphores. Data moves between devices by JAX's collectives and lax.ppermute only.
A program may use at most 128 MiB of HBM per device.

```python
import math
import jax
import jax.numpy as jnp
import numpy as np
from jax import lax

D = 768
FF = 3072
HEADS = 12
HEAD_DIM = 64
SEQ = 128
TOK_DEV = 256
EXPERTS = 8
CAP = 68
PAIRS = 32
N_WIDE = 8
N_NARROW = 4


def level_of(own_key, dims, cuts, smallest, top_value):
    factor_of, own = 1.0, jax.random.fold_in(own_key, 6)
    for position, parts in cuts:
        steps = jnp.exp(jax.random.uniform(jax.random.fold_in(own, position), (parts,), jnp.float32, smallest / len(cuts), top_value / len(cuts)))
        factor_of = factor_of * jnp.repeat(steps, dims[position] // parts).reshape([-1 if axis == position else 1 for axis in range(len(dims))])
    return factor_of


def deal_out(own_key, own, number, rows, number_of, top, most, slope):
    order = jax.random.permutation(own_key, number_of)
    crowded, usual = shares(number_of, rows * top, most, slope, True), shares(number_of, rows * top, most, slope, False)
    places = jnp.arange(number_of)

    def named(tallies, rotation):
        used = int((tallies > 0).sum())
        fixed = max(1, used // 4)
        shifted = fixed + (places - fixed + rotation * (used - fixed)) % max(1, number_of - fixed)
        return jnp.zeros((number_of,), jnp.int32).at[order[jnp.where(places < fixed, places, shifted)]].set(jnp.asarray(tallies, jnp.int32))

    tallies = jnp.where(number % 4 == 0, named(crowded, number // 4), named(usual, number - number // 4 - 1))
    mixed = jax.random.permutation(jax.random.fold_in(own, 3), number_of)
    donor, receiver = mixed[0:number_of // 2 * 2:2], mixed[1:number_of // 2 * 2:2]
    margin = jnp.minimum(tallies[donor] - 1, most - tallies[receiver]) // 2
    margin = jnp.where((donor == order[0]) | (receiver == order[0]) | (tallies[receiver] == 0), 0, jnp.maximum(margin, 0))
    shifted = jax.random.randint(jax.random.fold_in(own, 4), (number_of // 2,), 0, 1 << 20) % (margin + 1)
    tallies = tallies.at[donor].add(-shifted).at[receiver].add(shifted)
    items = jnp.searchsorted(jnp.cumsum(tallies), jnp.arange(rows * top), side="right").astype(jnp.int32)
    grid = items.reshape(top, rows).T
    grid = grid[jax.random.permutation(jax.random.fold_in(own, 1), rows)]
    rotation = jax.random.randint(jax.random.fold_in(own, 2), (rows, 1), 0, top)
    return jnp.take_along_axis(grid, (jnp.arange(top)[None, :] + rotation) % top, axis=1)


def shares(number_of, total, most, slope, full):
    portions = [(1 << 20) // math.isqrt(grade ** slope) + 1 for grade in range(1, number_of + 1)]
    largest = most if full else min(most, max(-(-total // number_of), total * portions[0] // sum(portions)))
    least = 1 if total - largest >= number_of - 1 else 0
    counts, spare = [largest] + [least] * (number_of - 1), total - largest - least * (number_of - 1)
    while spare > 0:
        movable = [i for i in range(1, number_of) if counts[i] < largest] or [i for i in range(1, number_of) if counts[i] < most]
        pool, budget = sum([portions[i] for i in movable]), spare
        for i in movable:
            addition = min(most - counts[i], max(1, budget * portions[i] // pool), spare)
            counts[i] = counts[i] + addition
            spare = spare - addition
    return np.array(counts)


def gaussian(own_key, extent, scale, most, cuts=(), kind=jnp.bfloat16):
    gain = level_of(own_key, extent, cuts, -0.22, 0.18) if cuts else 1.0
    array = jax.random.normal(own_key, extent, jnp.float32) * scale * gain
    return jnp.minimum(jnp.maximum(array, -most), most).astype(kind)


def setup_inputs(seed: int = 0) -> dict:
    seeds = jax.random.split(jax.random.key(seed), 9)
    pair_tokens = gaussian(seeds[0], (PAIRS, 2, SEQ, D), 1.0, 6.0, ((0, 32),))
    expert_ids_keys = jax.random.split(jax.random.fold_in(seeds[1], 1), PAIRS * (2 * SEQ) // TOK_DEV)
    expert_ids_turns = jax.random.permutation(jax.random.fold_in(seeds[1], 3), PAIRS * (2 * SEQ) // TOK_DEV)
    expert_ids = jax.vmap(lambda own, number: deal_out(jax.random.fold_in(seeds[1], 2), own, number, TOK_DEV, EXPERTS, 2, CAP, 1))(expert_ids_keys, expert_ids_turns).reshape((PAIRS, 2 * SEQ, 2))
    positive = jax.random.permutation(seeds[2], PAIRS).astype(jnp.int32)
    w_qkv = gaussian(seeds[3], (D, 3 * D), D ** -0.5, 0.21875)
    w_out = gaussian(seeds[4], (D, D), D ** -0.5, 0.21875)
    w_router = gaussian(seeds[5], (D, EXPERTS), D ** -0.5, 0.21875)
    w_up = gaussian(seeds[6], (EXPERTS, D, FF), D ** -0.5, 0.21875, ((0, 8), (2, 4)))
    w_down = gaussian(seeds[7], (EXPERTS, FF, D), FF ** -0.5, 0.109375, ((0, 8), (1, 4)))
    return {"pair_tokens": pair_tokens, "expert_ids": expert_ids, "positive": positive, "w_qkv": w_qkv, "w_out": w_out, "w_router": w_router, "w_up": w_up, "w_down": w_down}


epsilon = 1e-06
inverse_softmax_warmth = 20.0
loss_scale = 64.0

def rms_scaled(values):
    return values * lax.rsqrt(lax.optimization_barrier(jnp.mean(values * values, axis=-1, keepdims=True)) + epsilon)

def attention_block(tokens, w_qkv, w_out):
    count = tokens.shape[0]
    width = tokens.shape[1]
    normed = rms_scaled(tokens.astype(jnp.float32)).astype(jnp.bfloat16)
    project = jnp.dot(normed, w_qkv, preferred_element_type=jnp.float32)
    project = project.reshape(count // SEQ, SEQ, 3, HEADS, HEAD_DIM)
    query = rms_scaled(project[:, :, 0]).astype(jnp.bfloat16)
    keys_normed = rms_scaled(project[:, :, 1]).astype(jnp.bfloat16)
    values_cast = project[:, :, 2].astype(jnp.bfloat16)
    cosine_logit_matrix = jnp.einsum('sqhe,skhe->shqk', query.astype(jnp.float32), keys_normed.astype(jnp.float32)) / math.sqrt(HEAD_DIM)
    weights = jnp.exp(cosine_logit_matrix)
    weights = (weights / lax.optimization_barrier(jnp.sum(weights, axis=-1, keepdims=True))).astype(jnp.bfloat16)
    mixed = jnp.einsum('shqk,skhe->sqhe', weights.astype(jnp.float32), values_cast.astype(jnp.float32))
    mixed = mixed.astype(jnp.bfloat16).reshape(count, width)
    update = jnp.dot(mixed, w_out, preferred_element_type=jnp.float32)
    return (tokens.astype(jnp.float32) + update).astype(jnp.bfloat16)

def gate_pair(logits, picks):
    experts = logits.shape[-1]
    onehot = (picks[:, :, None] == jnp.arange(experts, dtype=jnp.int32)[None, None, :]).astype(jnp.float32)
    chosen_logits = lax.optimization_barrier(jnp.sum(onehot * logits[:, None, :], axis=-1))
    first = jax.nn.sigmoid(chosen_logits[:, 0] - chosen_logits[:, 1])
    return jnp.stack([first, 1.0 - first], axis=1)

def slot_positions(picks, experts, capacity):
    flat = picks.reshape(-1).astype(jnp.int32)
    onehot = (flat[:, None] == jnp.arange(experts, dtype=jnp.int32)[None, :]).astype(jnp.int32)
    earlier = jnp.cumsum(onehot, axis=0) - onehot
    return flat * capacity + lax.optimization_barrier(jnp.sum(earlier * onehot, axis=1)).astype(jnp.int32)

def reference(pair_tokens, expert_ids, positive, w_qkv, w_out, w_router, w_up, w_down):
    devices = N_WIDE * N_NARROW
    total = devices * TOK_DEV
    blocks_in = pair_tokens.reshape(devices, TOK_DEV, D)
    picks_in = expert_ids.reshape(devices, TOK_DEV, 2)

    def front(pieces):
        block, picks = pieces
        hidden_state = attention_block(block, w_qkv, w_out)
        normed = rms_scaled(hidden_state.astype(jnp.float32)).astype(jnp.bfloat16)
        logits = jnp.dot(normed, w_router, preferred_element_type=jnp.float32)
        gates = gate_pair(logits, picks)
        destination = slot_positions(picks, EXPERTS, CAP)
        return (hidden_state, normed, gates, destination)
    hidden_state, normed, gates, destination = lax.map(front, (blocks_in, picks_in))
    device_index = jnp.arange(devices, dtype=jnp.int32)[:, None]
    global_row = destination // CAP * (devices * CAP) + device_index * CAP + destination % CAP
    source = device_index * TOK_DEV + jnp.arange(2 * TOK_DEV, dtype=jnp.int32)[None, :] // 2
    table = jnp.full((EXPERTS * devices * CAP,), total, dtype=jnp.int32)
    table = table.at[global_row.reshape(-1)].set(source.reshape(-1).astype(jnp.int32))
    table = table.reshape(EXPERTS, devices * CAP)
    padded = jnp.concatenate([normed.reshape(total, D), jnp.zeros((1, D), normed.dtype)], axis=0)
    block_width = FF // N_NARROW

    def expert_forward(pieces):
        index, up_weight, down_weight = pieces
        slot_rows = padded[index]
        pre_act = jnp.dot(slot_rows, up_weight, preferred_element_type=jnp.float32)
        activated = jax.nn.gelu(pre_act).astype(jnp.bfloat16)
        split = activated.reshape(-1, N_NARROW, block_width).astype(jnp.float32)
        downs = down_weight.reshape(N_NARROW, block_width, D).astype(jnp.float32)
        partial_value = jnp.einsum('rnf,nfd->nrd', split, downs)
        rounded = lax.optimization_barrier(partial_value.astype(jnp.bfloat16))
        return lax.optimization_barrier(jnp.sum(rounded.astype(jnp.float32), axis=0)).astype(jnp.bfloat16)
    expert_out = lax.map(expert_forward, (table, w_up, w_down)).reshape(EXPERTS * devices * CAP, D)
    picked = expert_out[global_row.reshape(-1)].reshape(devices, TOK_DEV, 2, D)
    mixed = hidden_state.astype(jnp.float32) + lax.optimization_barrier(jnp.sum(gates[:, :, :, None] * picked.astype(jnp.float32), axis=2))
    pooled = lax.optimization_barrier(jnp.mean(mixed.reshape(PAIRS, 2, SEQ, D), axis=2))
    length = jnp.sqrt(lax.optimization_barrier(jnp.sum(pooled * pooled, axis=-1, keepdims=True)) + epsilon)
    unit = pooled / length
    search_unit_vector = unit[:, 0]
    passage_unit_vector = unit[:, 1]
    cosine_logit_matrix = jnp.dot(search_unit_vector, passage_unit_vector.T, precision=lax.Precision.HIGHEST) * inverse_softmax_warmth
    probs = jnp.exp(cosine_logit_matrix)
    probs = probs / lax.optimization_barrier(jnp.sum(probs, axis=1, keepdims=True))
    target = (positive[:, None] == jnp.arange(PAIRS, dtype=jnp.int32)[None, :]).astype(jnp.float32)
    logit_excess_matrix = (probs - target) * loss_scale
    search_embedding_adjoint = jnp.dot(logit_excess_matrix, passage_unit_vector, precision=lax.Precision.HIGHEST) * inverse_softmax_warmth
    passage_embedding_adjoint = jnp.dot(logit_excess_matrix.T, search_unit_vector, precision=lax.Precision.HIGHEST) * inverse_softmax_warmth
    unit_grad = jnp.stack([search_embedding_adjoint, passage_embedding_adjoint], axis=1)
    pooled_grad = (unit_grad - unit * lax.optimization_barrier(jnp.sum(unit * unit_grad, axis=-1, keepdims=True))) / length
    token_grad = jnp.broadcast_to((pooled_grad / SEQ)[:, :, None, :], (PAIRS, 2, SEQ, D)).reshape(devices, TOK_DEV, D)
    cotangent = (gates[:, :, :, None] * token_grad[:, :, None, :]).astype(jnp.bfloat16).reshape(-1, D)
    cot_table = jnp.zeros((EXPERTS * devices * CAP, D), jnp.bfloat16).at[global_row.reshape(-1)].set(cotangent)
    cot_table = cot_table.reshape(EXPERTS, devices * CAP, D)

    def expert_backward(pieces):
        index, up_weight, down_weight, grad_rows = pieces
        slot_rows = padded[index]
        pre_act = jnp.dot(slot_rows, up_weight, preferred_element_type=jnp.float32)
        activated = jax.nn.gelu(pre_act).astype(jnp.bfloat16)
        down_grad = jnp.dot(activated.T, grad_rows, preferred_element_type=jnp.float32)
        act_grad = jnp.dot(grad_rows, down_weight.T, preferred_element_type=jnp.float32)
        unused, pullback = jax.vjp(jax.nn.gelu, pre_act)
        pre_grad = pullback(act_grad)[0].astype(jnp.bfloat16)
        up_grad = jnp.dot(slot_rows.T, pre_grad, preferred_element_type=jnp.float32)
        return (up_grad, down_grad)
    grad_up, grad_down = lax.map(expert_backward, (table, w_up, w_down, cot_table))
    return (grad_up, grad_down)
```

```python
import functools

import jax
import jax.numpy as jnp
from jax import lax
from jax.experimental import pallas as pl
from jax.experimental.pallas import tpu as pltpu
from jax.sharding import PartitionSpec as P

HEADS = 12
HEAD_DIM = 64
SEQ = 128
EPS = 1e-06
WARMTH = 20.0
LOSS_SCALE = 64.0
LANES = 128
INFO = 8
SELECT_WEIGHT = 1000
GELU_C = 0.7978845608028654
GELU_D = 0.044715 * GELU_C
BF16 = jnp.bfloat16
F32 = jnp.float32


def dot(left, right, contract=(1, 0)):
    return lax.dot_general(
        left, right, (((contract[0],), (contract[1],)), ((), ())), preferred_element_type=F32
    )


def split_dot(left, right, contract):
    left_high, right_high = left.astype(BF16), right.astype(BF16)
    left_low = (left - left_high.astype(F32)).astype(BF16)
    right_low = (right - right_high.astype(F32)).astype(BF16)
    return (
        dot(left_low, right_high, contract) + dot(left_high, right_low, contract)
    ) + dot(left_high, right_high, contract)


def iota(shape, axis):
    return lax.broadcasted_iota(jnp.int32, shape, axis)


def rms_scaled(values):
    return values * lax.rsqrt(jnp.mean(values * values, axis=-1, keepdims=True) + EPS)


def dispatch(rows, info, experts, block, capacity):
    count = rows.shape[0]
    first, second, slot_a, slot_b, gate_a, gate_b = (info[i : i + 1] for i in range(6))
    place = iota((experts * block, count), 0).astype(F32)
    chosen = (place == first * block + slot_a) | (place == second * block + slot_b)
    out = dot(jnp.where(chosen, 1.0, 0.0).astype(BF16), rows)
    expert = iota((experts, count), 0).astype(F32)
    owned = jnp.concatenate(
        [jnp.where(expert == first, gate_a, 0.0), jnp.where(expert == second, gate_b, 0.0)], axis=1
    ).astype(BF16)
    lane = iota((LANES, count), 0).astype(F32)
    slots = jnp.concatenate(
        [jnp.where(lane == slot_a, 1.0, 0.0), jnp.where(lane == slot_b, 1.0, 0.0)], axis=1
    ).astype(BF16)
    gates = dot(owned, slots, (1, 1))
    gate_row = iota((block, LANES), 0) == capacity
    blocks = []
    for e in range(experts):
        part = out[e * block : (e + 1) * block]
        head = jnp.where(gate_row, gates[e : e + 1], part[:, :LANES])
        blocks.append(jnp.concatenate([head, part[:, LANES:]], axis=1))
    return blocks


def front_kernel(
    tokens_hbm, ids_hbm, router_hbm, qkv_hbm, out_hbm,
    half_ref, whole_ref, sums_ref,
    tokens_ref, ids_ref, router_ref, qkv_ref, w_out_ref, mixed_ref, sems,
):
    count, width = tokens_ref.shape
    parts = [
        pltpu.make_async_copy(
            qkv_hbm.at[:, pl.ds(i * width, width)], qkv_ref.at[i], sems.at[i]
        )
        for i in range(3)
    ]
    last = pltpu.make_async_copy(out_hbm, w_out_ref, sems.at[3])
    first = pltpu.make_async_copy(tokens_hbm, tokens_ref, sems.at[4])
    small = [
        pltpu.make_async_copy(ids_hbm, ids_ref, sems.at[5]),
        pltpu.make_async_copy(router_hbm, router_ref, sems.at[6]),
    ]
    for load in [first, *parts, last, *small]:
        load.start()
    first.wait()
    tokens = tokens_ref[...].astype(F32)
    normed = rms_scaled(tokens).astype(BF16)
    half = iota((SEQ, LANES), 1) < HEAD_DIM
    wide = 2 * LANES
    same_head = jnp.where(
        iota((wide, wide), 0) // HEAD_DIM == iota((wide, wide), 1) // HEAD_DIM, 1.0, 0.0
    ).astype(BF16)

    def head_scaled(part, scale):
        out = []
        for start in range(0, width, wide):
            some = part[:, start : start + wide]
            squares = some * some
            high = squares.astype(BF16)
            low = (squares - high.astype(F32)).astype(BF16)
            level = dot(high, same_head) + dot(low, same_head)
            out.append(some * (lax.rsqrt(level * (1.0 / HEAD_DIM) + EPS) * scale))
        return jnp.concatenate(out, axis=1)

    parts[0].wait()
    query = head_scaled(dot(normed, qkv_ref[0]), HEAD_DIM ** -0.5)
    parts[1].wait()
    keys = head_scaled(dot(normed, qkv_ref[1]), 1.0).astype(BF16)
    parts[2].wait()
    values = dot(normed, qkv_ref[2]).astype(BF16)
    ones = jnp.ones((SEQ, LANES), BF16)
    pieces = [
        (slice(seq * SEQ, (seq + 1) * SEQ), slice(start, start + LANES))
        for start in range(0, width, LANES)
        for seq in range(count // SEQ)
    ]
    scores = []
    for at in pieces:
        one = query[at]
        both = jnp.concatenate([jnp.where(half, one, 0.0), jnp.where(half, 0.0, one)], axis=0)
        scores.append(dot(both.astype(BF16), keys[at], (1, 1)))
    weights = [jnp.exp(score).astype(BF16) for score in scores]
    summed = [
        dot(weight, jnp.concatenate([values[at], ones], axis=1))
        for at, weight in zip(pieces, weights)
    ]
    for at, both in zip(pieces, summed):
        shares = both[:, :LANES] / both[:, LANES:]
        mixed_ref[at] = jnp.where(half, shares[:SEQ], shares[SEQ:]).astype(BF16)
    last.wait()
    hidden = (tokens + dot(mixed_ref[...], w_out_ref[...])).astype(BF16).astype(F32)
    for seq in range(count // SEQ):
        sums_ref[seq : seq + 1] = jnp.sum(
            hidden[seq * SEQ : (seq + 1) * SEQ], axis=0, keepdims=True
        )
    normed = rms_scaled(hidden).astype(BF16)
    for load in small:
        load.wait()
    logits = dot(router_ref[...], normed, (1, 1))
    ids = ids_ref[...]
    expert = iota(logits.shape, 0)
    named_a = jnp.where(ids[0:1] == expert, 1.0, 0.0)
    named_b = jnp.where(ids[1:2] == expert, 1.0, 0.0)
    logit_a = jnp.sum(named_a * logits, axis=0, keepdims=True)
    logit_b = jnp.sum(named_b * logits, axis=0, keepdims=True)
    gate_a = jax.nn.sigmoid(logit_a - logit_b)
    sign = jnp.where(iota((1, count), 1) < SEQ, 1.0, -1.0)
    earlier = jnp.where(iota((count, count), 0) < iota((count, count), 1), 1.0, 0.0).astype(BF16)
    before = dot((named_a + named_b).astype(BF16), earlier)
    info = jnp.concatenate(
        [
            ids.astype(F32),
            jnp.sum(named_a * before, axis=0, keepdims=True),
            jnp.sum(named_b * before, axis=0, keepdims=True),
            gate_a * sign,
            (1.0 - gate_a) * sign,
            jnp.zeros((INFO - 6, count), F32),
        ],
        axis=0,
    )
    for ref in (half_ref, whole_ref):
        near = ref.shape[1]
        tail = jnp.concatenate([info, jnp.zeros((INFO, near - count), F32)], axis=1)
        ref[...] = jnp.concatenate([normed[:, :near], tail.astype(BF16)], axis=0)


def own_kernel(experts, block, capacity, payload_ref, near_ref, far_ref):
    payload = payload_ref[...]
    count, half = payload.shape[0] - INFO, near_ref.shape[-1]
    info = payload[count:, :count].astype(F32)
    blocks = dispatch(payload[:count], info, experts, block, capacity)
    for e in range(experts):
        near_ref[e] = blocks[e][:, :half].astype(BF16)
        far_ref[e] = blocks[e][:, half:].astype(BF16)


def select_kernel(experts, block, capacity, *refs):
    steps = (len(refs) - 2) // 2
    shards, out_hbm, parts, sems = refs[:steps], refs[steps], refs[steps + 1 : -1], refs[-1]
    start, stores = 0, []
    for i, (shard_ref, part_ref) in enumerate(zip(shards, parts)):
        shard = shard_ref[...]
        count, near = shard.shape[0] - INFO, shard.shape[1]
        info = shard[count:, :count].astype(F32)
        blocks = dispatch(shard[:count], info, experts, block, capacity)
        for e in range(experts):
            part_ref[e] = blocks[e].astype(BF16)
        stores.append(
            pltpu.make_async_copy(part_ref, out_hbm.at[:, :, pl.ds(start, near)], sems.at[i])
        )
        stores[-1].start()
        start += near
    for store in stores:
        store.wait()


def gelu_parts(pre):
    square = pre * pre
    return square, jnp.tanh(pre * (GELU_C + GELU_D * square))


def gelu_slope(pre, square, turn):
    inner = pre * (GELU_C + 3.0 * GELU_D * square)
    return 0.5 * (1.0 + turn) + 0.5 * inner * (1.0 - turn * turn)


def gate_matrix(head, origin, experts, groups, block, capacity):
    devices = experts * groups
    column = iota((block, 2 * devices), 1)
    tile, row = capacity // 8 * 8, capacity % 8
    found = [
        head[w * block + tile : w * block + tile + 8][row : row + 1] for w in range(experts)
    ]
    found.append(jnp.zeros((LANES - experts, LANES), F32))
    turned = jnp.concatenate(found, axis=0).T[:block]
    pieces = []
    for w in range(experts):
        gate = turned[:, w : w + 1]
        device = w * groups + origin
        pieces.append(
            jnp.where(
                column == device,
                jnp.maximum(gate, 0.0),
                jnp.where(column == device + devices, jnp.maximum(-gate, 0.0), 0.0),
            )
        )
    return jnp.concatenate(pieces, axis=0).astype(BF16)


def shard_rows(near_ref):
    return jnp.concatenate(
        [near_ref[w].astype(F32) for w in range(near_ref.shape[0])], axis=0
    )


def own_expert_kernel(
    experts, groups, block, capacity,
    near_ref, far_ref, up_ref, slope_ref, gates_ref, sums_ref,
):
    pre = dot(jnp.concatenate([near_ref[...], far_ref[...]], axis=1), up_ref[...])
    square, turn = gelu_parts(pre)
    act = (0.5 * pre * (1.0 + turn)).astype(BF16)
    slope_ref[...] = gelu_slope(pre, square, turn).astype(BF16)
    head = near_ref[:, :LANES].astype(F32)
    gates = gate_matrix(head, lax.axis_index("narrow"), experts, groups, block, capacity)
    gates_ref[...] = gates
    sums_ref[...] = dot(gates, act, (0, 0))


def expert_kernel(experts, groups, block, capacity, nears, *refs):
    near_hbm = refs[0]
    count = groups - 1
    owners = [i for i in range(count) if nears[i] < max(nears)]
    far_hbms = refs[1 : 1 + len(owners)]
    (
        up_hbm, down_hbm, own_sums_hbm, pre_hbm, gates_hbm, sums_hbm, partial_hbm,
        partial_ref, up_ref, down_ref, pre_ref, gates_ref, sums_ref, *parts, sems,
    ) = refs[1 + len(owners) :]
    near_refs, far_refs = parts[:count], parts[count:]
    here = lax.axis_index("narrow")
    size = experts * block
    devices = experts * groups
    slots = iter(range(sems.shape[0]))

    def copy(source, target):
        return pltpu.make_async_copy(source, target, sems.at[next(slots)])

    weights = [copy(up_hbm, up_ref), copy(down_hbm, down_ref)]
    own_sums = copy(own_sums_hbm, sums_ref)
    loads = []
    for i in range(count):
        columns = pl.ds(sum(nears[:i]), nears[i])
        loads.append([copy(near_hbm.at[:, :, columns], near_refs[i])])
        if i in owners:
            loads[i].append(copy(far_hbms[owners.index(i)], far_refs[owners.index(i)]))
    ats = [pl.ds(i * size, size) for i in range(count)]
    stores = [copy(pre_ref.at[at], pre_hbm.at[at]) for at in ats]
    gate_stores = [copy(gates_ref.at[at], gates_hbm.at[at]) for at in ats]
    sums_store = copy(sums_ref, sums_hbm)
    partial_store = copy(partial_ref, partial_hbm)
    for load in [weights[0], *sum(loads, []), own_sums, weights[1]]:
        load.start()
    weights[0].wait()
    cuts = [slice(start, start + size // 2) for start in (0, size // 2)]
    for i in range(count):
        at = slice(i * size, (i + 1) * size)
        for load in loads[i]:
            load.wait()
        gathered = shard_rows(near_refs[i])
        rows = gathered.astype(BF16)
        if i in owners:
            rows = jnp.concatenate([rows, far_refs[owners.index(i)][...]], axis=1)
        acts = []
        for cut in cuts:
            pre = dot(rows[cut], up_ref[...])
            pre_ref[i * size + cut.start : i * size + cut.stop] = pre.astype(BF16)
            turn = gelu_parts(pre)[1]
            acts.append((0.5 * pre * (1.0 + turn)).astype(BF16))
        stores[i].start()
        act = jnp.concatenate(acts, axis=0)
        origin = lax.rem(here + count - i, groups)
        gates = gate_matrix(gathered[:, :LANES], origin, experts, groups, block, capacity)
        gates_ref[at] = gates
        gate_stores[i].start()
        part = dot(gates, act, (0, 0))
        if i == 0:
            own_sums.wait()
            total = sums_ref[...]
        total = total + part
    sums_ref[...] = total
    sums_store.start()
    high = total.astype(BF16)
    low = (total - high.astype(F32)).astype(BF16)
    weights[1].wait()
    pooled = dot(jnp.concatenate([high, low], axis=0), down_ref[...])
    pooled = pooled[: 2 * devices] + pooled[2 * devices :]
    for device in range(devices):
        pair = [pooled[i : i + 1] for i in (device, device + devices)]
        partial_ref[device] = jnp.concatenate(pair, axis=0).astype(BF16)
    partial_store.start()
    for store in [*stores, *gate_stores, sums_store, partial_store]:
        store.wait()


def slope_kernel(pre_hbm, slope_hbm, pre_ref, slope_ref, sems):
    parts = sems.shape[1]
    size = pre_ref.shape[0] // parts
    cuts = [pl.ds(i * size, size) for i in range(parts)]
    loads = [
        pltpu.make_async_copy(pre_hbm.at[cut], pre_ref.at[cut], sems.at[0, i])
        for i, cut in enumerate(cuts)
    ]
    stores = [
        pltpu.make_async_copy(slope_ref.at[cut], slope_hbm.at[cut], sems.at[1, i])
        for i, cut in enumerate(cuts)
    ]
    for load in loads:
        load.start()
    for cut, load, store in zip(cuts, loads, stores):
        load.wait()
        pre = pre_ref[cut].astype(F32)
        slope_ref[cut] = gelu_slope(pre, *gelu_parts(pre)).astype(BF16)
        store.start()
    for store in stores:
        store.wait()


def turn_kernel(nears, *refs):
    count = len(nears)
    owners = [i for i in range(count) if nears[i] < max(nears)]
    hbms, (turned_hbm, *refs) = refs[: 3 + len(owners)], refs[3 + len(owners) :]
    refs, turned_ref, sems = refs[: len(hbms)], refs[-2], refs[-1]
    loads = [
        pltpu.make_async_copy(hbm, ref, sems.at[i]) for i, (hbm, ref) in enumerate(zip(hbms, refs))
    ]
    for load in loads:
        load.start()
    near_ref, far_refs = refs[2], refs[3:]
    size = refs[0].shape[0]
    stores = []
    loads[0].wait()
    loads[1].wait()
    rows = jnp.concatenate([refs[0][...], refs[1][...]], axis=1)
    turned_ref[:, :size] = rows.T
    loads[2].wait()
    for i, near in enumerate(nears, 1):
        start = sum(nears[: i - 1])
        rows = jnp.concatenate(
            [near_ref[w, :, start : start + near].astype(F32) for w in range(near_ref.shape[0])],
            axis=0,
        ).astype(BF16)
        if i - 1 in owners:
            loads[3 + owners.index(i - 1)].wait()
            rows = jnp.concatenate([rows, far_refs[owners.index(i - 1)][...]], axis=1)
        turned_ref[:, i * size : (i + 1) * size] = rows.T
        if i % 2:
            cut = pl.ds((i - 1) * size, 2 * size)
            stores.append(
                pltpu.make_async_copy(
                    turned_ref.at[:, cut], turned_hbm.at[:, cut], sems.at[len(hbms) + i // 2]
                )
            )
            stores[-1].start()
    for store in stores:
        store.wait()


def pool_kernel(parts_ref, own_ref, out_ref):
    total = (jnp.sum(parts_ref[...].astype(F32), axis=0) + own_ref[...]) * (1.0 / SEQ)
    out_ref[...] = jnp.broadcast_to(total.astype(BF16)[None], out_ref.shape)


def backward_kernel(
    pooled_hbm, positive_hbm, gates_own_hbm, gates_hbm, sums_hbm, down_w_hbm,
    turned_hbm, slope_own_hbm, slope_hbm, up_hbm, down_hbm,
    pooled_ref, positive_ref, gates_ref, sums_ref, down_ref, turned_ref, slope_ref, pre_grad_ref, up_grad_ref, down_grad_ref, sems,
):
    width = down_ref.shape[1]
    devices = pooled_ref.shape[0]
    size = slope_own_hbm.shape[0]
    total = slope_ref.shape[0]
    loads = [
        pltpu.make_async_copy(slope_own_hbm, slope_ref.at[pl.ds(0, size)], sems.at[0]),
        pltpu.make_async_copy(slope_hbm, slope_ref.at[pl.ds(size, total - size)], sems.at[1]),
        pltpu.make_async_copy(turned_hbm, turned_ref, sems.at[2]),
        pltpu.make_async_copy(down_w_hbm, down_ref, sems.at[3]),
        pltpu.make_async_copy(sums_hbm, sums_ref, sems.at[4]),
        pltpu.make_async_copy(gates_own_hbm, gates_ref.at[pl.ds(0, size)], sems.at[5]),
        pltpu.make_async_copy(gates_hbm, gates_ref.at[pl.ds(size, total - size)], sems.at[6]),
    ]
    count = sems.shape[0]
    first = [
        pltpu.make_async_copy(pooled_hbm, pooled_ref, sems.at[count - 2]),
        pltpu.make_async_copy(positive_hbm, positive_ref, sems.at[count - 1]),
    ]
    for load in [*first, *loads[3:], *loads[:3]]:
        load.start()
    for load in first:
        load.wait()

    def unit_of(pooled):
        length = jnp.sqrt(jnp.sum(pooled * pooled, axis=1, keepdims=True) + EPS)
        return pooled / length, length

    pooled = pooled_ref[...].astype(F32)
    query, query_length = unit_of(pooled[:, 0])
    document, document_length = unit_of(pooled[:, 1])
    powers = jnp.exp(split_dot(query, document, (1, 1)) * WARMTH)
    probs = powers / jnp.sum(powers, axis=1, keepdims=True)
    row, column = iota((devices, devices), 0), iota((devices, devices), 1)
    chosen = jnp.where(positive_ref[...] == row, 1.0, 0.0).astype(BF16)
    target = dot(jnp.where(row == column, 1.0, 0.0).astype(BF16), chosen, (1, 1))
    excess = (probs - target) * LOSS_SCALE
    query_grad = split_dot(excess, document, (1, 0)) * WARMTH
    document_grad = split_dot(excess, query, (0, 0)) * WARMTH

    def pooled_grad(unit, grad, length):
        return (grad - unit * jnp.sum(unit * grad, axis=1, keepdims=True)) / (length * SEQ)

    token_grad = jnp.concatenate(
        [
            pooled_grad(query, query_grad, query_length),
            pooled_grad(document, document_grad, document_length),
        ],
        axis=0,
    ).astype(BF16)
    loads[3].wait()
    loads[4].wait()
    hidden_grad = dot(token_grad, down_ref[...], (1, 1)).astype(BF16)
    down_grad_ref[...] = dot(sums_ref[...].astype(BF16), token_grad, (0, 0))
    stores = [pltpu.make_async_copy(down_grad_ref, down_hbm, sems.at[7])]
    stores[0].start()
    for i in (5, 6, 0, 1):
        loads[i].wait()
    for start in range(0, total, size // 2):
        at = slice(start, start + size // 2)
        act_grad = dot(gates_ref[at], hidden_grad)
        pre_grad_ref[at] = (act_grad * slope_ref[at].astype(F32)).astype(BF16)
    loads[2].wait()
    tile = column_tile(pre_grad_ref.shape[1])
    for i, start in enumerate(range(0, pre_grad_ref.shape[1], tile)):
        cols = slice(start, start + tile)
        up_grad_ref[:, cols] = dot(turned_ref[...], pre_grad_ref[:, cols])
        store = pltpu.make_async_copy(
            up_grad_ref.at[:, pl.ds(start, tile)],
            up_hbm.at[:, pl.ds(start, tile)],
            sems.at[8 + i],
        )
        store.start()
        stores.append(store)
    for store in stores:
        store.wait()


MIB = 1024 * 1024


def column_tile(size):
    return 2 * LANES if size % (2 * LANES) == 0 else LANES


def call(kernel, outs, args, spaces, out_spaces=None, scratch=(), flops=0, vmem=60):
    outs = tuple(jax.ShapeDtypeStruct(s, d) for s, d in outs)
    out_spaces = out_spaces or "v" * len(outs)
    space = {"v": pltpu.VMEM, "s": pltpu.SMEM, "a": pl.ANY}
    moved = sum(x.size * jnp.dtype(x.dtype).itemsize for x in tuple(args) + outs)
    return pl.pallas_call(
        kernel,
        out_shape=outs,
        in_specs=[pl.BlockSpec(memory_space=space[k]) for k in spaces],
        out_specs=tuple(pl.BlockSpec(memory_space=space[k]) for k in out_spaces),
        scratch_shapes=[pltpu.VMEM(*x) if isinstance(x, tuple) else x for x in scratch],
        compiler_params=pltpu.CompilerParams(vmem_limit_bytes=vmem * MIB),
        cost_estimate=pl.CostEstimate(flops=flops, bytes_accessed=moved, transcendentals=0),
    )(*args)


def body(pair_tokens, expert_ids, positive, w_qkv, w_out, w_router, w_up, w_down):
    experts = lax.axis_size("wide")
    groups = lax.axis_size("narrow")
    devices = experts * groups
    width = pair_tokens.shape[-1]
    tokens = pair_tokens.reshape(-1, width)
    count = tokens.shape[0]
    capacity = 17 * count // (8 * experts)
    block = -(-(capacity + 1) // 8) * 8
    half = width // 2
    nears = [width if 2 * step == groups else half for step in range(1, groups)]
    size = experts * block
    hidden = w_up.shape[2]
    up, down = w_up[0], w_down[0]

    def from_behind(array, step):
        return lax.ppermute(array, "narrow", [(i, (i + step) % groups) for i in range(groups)])

    payload_half, payload, own_sum = call(
        front_kernel,
        [((count + INFO, half), BF16), ((count + INFO, width), BF16), ((2, width), F32)],
        (tokens, expert_ids.reshape(-1, 2).T, w_router.T, w_qkv, w_out),
        "aaaaa",
        scratch=[
            ((count, width), BF16),
            ((2, count), jnp.int32),
            ((experts, width), BF16),
            ((3, width, width), BF16),
            ((width, width), BF16),
            ((count, width), BF16),
            pltpu.SemaphoreType.DMA((7,)),
        ],
        flops=2 * count * width * width * 5,
    )
    shards = [
        from_behind(payload if near == width else payload_half, step)
        for step, near in enumerate(nears, 1)
    ]
    own_halves = call(
        functools.partial(own_kernel, experts, block, capacity),
        [((experts, block, half), BF16), ((experts, block, width - half), BF16)],
        (payload,),
        "v",
        flops=2 * size * count * width,
    )
    own_far, own_near = (
        lax.all_to_all(x, "wide", split_axis=0, concat_axis=0, tiled=True).reshape(size, -1)
        for x in own_halves[::-1]
    )
    (near_out,) = call(
        functools.partial(select_kernel, experts, block, capacity),
        [((experts, block, sum(nears)), BF16)],
        shards,
        "v" * (groups - 1),
        "a",
        scratch=[
            *(((experts, block, near), BF16) for near in nears),
            pltpu.SemaphoreType.DMA((groups - 1,)),
        ],
        flops=SELECT_WEIGHT * 2 * size * count * sum(nears),
        vmem=24,
    )
    near_out, far_sent = lax.optimization_barrier((near_out, own_far))
    far_rows = [
        from_behind(far_sent, step) for step, near in enumerate(nears, 1) if near < width
    ]
    near_rows = lax.all_to_all(near_out, "wide", split_axis=0, concat_axis=0, tiled=True)

    total = groups * size
    slope_own, gates_own, sums_own = call(
        functools.partial(own_expert_kernel, experts, groups, block, capacity),
        [((size, hidden), BF16), ((size, 2 * devices), BF16), ((2 * devices, hidden), F32)],
        (own_near, own_far, up),
        "vvv",
        flops=2 * size * width * hidden,
        vmem=64,
    )
    pre, gates, sums, partial = call(
        functools.partial(expert_kernel, experts, groups, block, capacity, nears),
        [
            ((total - size, hidden), BF16),
            ((total - size, 2 * devices), BF16),
            ((2 * devices, hidden), F32),
            ((devices, 2, width), BF16),
        ],
        (near_rows, *far_rows, up, down, sums_own),
        "a" * (4 + len(far_rows)),
        "aaaa",
        scratch=[
            ((devices, 2, width), BF16),
            ((width, hidden), BF16),
            ((hidden, width), BF16),
            ((total - size, hidden), BF16),
            ((total - size, 2 * devices), BF16),
            ((2 * devices, hidden), F32),
            *(((experts, block, near), BF16) for near in nears),
            *(((size, width - near), BF16) for near in nears if near < width),
            pltpu.SemaphoreType.DMA((5 + 4 * (groups - 1),)),
        ],
        flops=2 * (total - size) * width * hidden,
    )
    axes = ("wide", "narrow")
    parts = lax.all_to_all(partial, axes, split_axis=0, concat_axis=0, tiled=True)
    (slope,) = call(
        slope_kernel,
        [((total - size, hidden), BF16)],
        (pre,),
        "a",
        "a",
        scratch=[
            ((total - size, hidden), BF16),
            ((total - size, hidden), BF16),
            pltpu.SemaphoreType.DMA((2, 2 * (groups - 1))),
        ],
        flops=total * hidden * 400,
    )
    parts, slope = lax.optimization_barrier((parts, slope))
    (pooled,) = call(pool_kernel, [((devices, 2, width), BF16)], (parts, own_sum), "vv", vmem=8)
    own_near, near_rows, pooled = lax.optimization_barrier((own_near, near_rows, pooled))
    pooled = lax.all_to_all(pooled, axes, split_axis=0, concat_axis=0, tiled=True)
    sources = (own_near, own_far, near_rows, *far_rows)
    (turned,) = call(
        functools.partial(turn_kernel, nears),
        [((width, total), BF16)],
        sources,
        "a" * len(sources),
        "a",
        scratch=[
            *((x.shape, BF16) for x in sources),
            ((width, total), BF16),
            pltpu.SemaphoreType.DMA((len(sources) + groups // 2,)),
        ],
        flops=total * hidden * 400,
        vmem=64,
    )
    up_grad, down_grad = call(
        backward_kernel,
        [((width, hidden), F32), ((hidden, width), F32)],
        (
            pooled, positive.reshape(1, devices), gates_own, gates, sums, down,
            turned, slope_own, slope,
        ),
        "aaaaaaaaa",
        "aa",
        scratch=[
            ((devices, 2, width), BF16),
            ((1, devices), jnp.int32),
            ((total, 2 * devices), BF16),
            ((2 * devices, hidden), F32),
            ((hidden, width), BF16),
            ((width, total), BF16),
            ((total, hidden), BF16),
            ((total, hidden), BF16),
            ((width, hidden), F32),
            ((hidden, width), F32),
            pltpu.SemaphoreType.DMA((10 + hidden // column_tile(hidden),)),
        ],
        flops=2 * total * width * hidden,
    )
    return (up_grad[None], down_grad[None])


def solution(mesh):
    return jax.shard_map(
        body,
        mesh=mesh,
        in_specs=(
            P(("wide", "narrow"), None, None, None),
            P(("wide", "narrow"), None, None),
            P(),
            P(),
            P(),
            P(),
            P("wide", None, "narrow"),
            P("wide", "narrow", None),
        ),
        out_specs=(P("wide", None, "narrow"), P("wide", "narrow", None)),
        check_vma=False,
    )
```
